32 devices in a mesh: seq: 16 (over z, y, core), tensor: 2 (over x).
Axes of the slice: x: 2, y: 2, z: 4, core: 2. Of those that a mesh axis runs over, the one named last changes fastest.
Arguments:
- tokens: bfloat16 [4096, 2048], P('seq'), may hold values from -6 to 6
- cotangent: bfloat16 [4096, 2048], P('seq'), may hold values from -6 to 6
- norm_gains: float32 [2, 2048], replicated, may hold values from 0.5 to 1.5
- mix_weight: bfloat16 [2048, 5, 2048], P('seq', None, 'tensor'), may hold values from -0.125 to 0.125
- rate_weight: bfloat16 [2048, 2, 16], P('seq', None, 'tensor'), may hold values from -0.125 to 0.125
- feed_weight: bfloat16 [2048, 3, 5632], P('seq', None, 'tensor'), may hold values from -0.125 to 0.125
- conv_weight: float32 [4, 3, 2048], P(None, None, 'tensor'), may hold values from -0.8 to 0.8
- decay_log: float32 [16], P('tensor'), may hold values from 0 to 2.77
- decay_bias: float32 [16], P('tensor'), may hold values from -6.9 to -2.3
- head_gain: float32 [16, 128], P('tensor'), may hold values from 0.5 to 1.5
- doc_starts: int32 [1, 6], replicated, may hold values from 0 to 4095, as said below
Outputs:
- block_out: bfloat16 [4096, 2048], P('seq')
- token_gradient: float32 [4096, 2048], P('seq')
- gains_gradient: float32 [2, 2048], replicated
- mix_gradient: float32 [2048, 5, 2048], P('seq', None, 'tensor')
- rate_gradient: float32 [2048, 2, 16], P('seq', None, 'tensor')
- feed_gradient: float32 [2048, 3, 5632], P('seq', None, 'tensor')
- conv_gradient: float32 [4, 3, 2048], P(None, None, 'tensor')
- decay_log_gradient: float32 [16], P('tensor')
- decay_bias_gradient: float32 [16], P('tensor')
- head_gain_gradient: float32 [16, 128], P('tensor')
The draws below stay inside these ranges and needn't reach their ends.
Inputs may be any that keep to these rules, and one draw needn't show every extreme that they name: Row s of doc_starts gives the documents of packed sequence s, counted from its first token; each row rises strictly and starts at 0, and document i of a row runs to the token before the next start, the last one to the sequence's end. In every row one document begins among the first 256 tokens of the sequence and ends among its last 256; every other start lies among the first or the last 256 tokens of the sequence.
All inputs are finite; a program needn't handle non-finite values.
Results may differ from the reference program's by a relative error of at most 0.023.
Values may be sent and summed in bfloat16 or wider, within the bound.
No kernel may reach another device: no remote copies, remote signals or barrier semaphores. Data moves between devices by JAX's collectives and lax.ppermute only.
A program may use at most 280 MiB of HBM per device.

```python
from functools import partial
import jax
import jax.numpy as jnp
from jax import lax

D = 2048
H = 16
DK = 128
FF = 5632
CONV = 4
GROUP = 64
DOCS = 6
TOK_DEV = 256
HK = 2048
TOKENS = 4096
SEQLEN = 4096
NSEQS = 1


def draw_doc_starts(key, part):
    key = jax.random.fold_in(key, 11)
    rows_key, pick_key = jax.random.split(key)

    def one_row(row_key):
        count_key, head_key, tail_key = jax.random.split(row_key, 3)
        head_count = jax.random.randint(count_key, (), 1, DOCS - 1)
        head = jnp.sort(jax.random.permutation(head_key, TOK_DEV - 1)[:DOCS - 2]).astype(jnp.int32) + 1
        tail_rows = jnp.sort(jax.random.permutation(tail_key, TOK_DEV - 2)[:DOCS - 2]).astype(jnp.int32) + (SEQLEN - TOK_DEV + 1)
        places = jnp.arange(1, DOCS, dtype=jnp.int32)
        head_pick = head[jnp.clip(places - 1, 0, DOCS - 3)]
        tail_pick = tail_rows[jnp.clip(places - 2, 0, DOCS - 3)]
        starts = jnp.where(places <= head_count, head_pick, tail_pick)
        return jnp.concatenate([jnp.zeros((1,), jnp.int32), starts]).astype(jnp.int32)
    rows = jax.vmap(one_row)(jax.random.split(rows_key, NSEQS))
    chosen = jax.random.randint(pick_key, (), 0, NSEQS)
    last = jnp.where(jnp.arange(NSEQS, dtype=jnp.int32) == chosen, SEQLEN - 1, rows[:, DOCS - 1])
    return rows.at[:, DOCS - 1].set(last.astype(jnp.int32)).astype(jnp.int32)


def levels(rng, shape, shards, smallest, largest):
    level, own = 1.0, jax.random.fold_in(rng, 6)
    for dim, shards_of in shards:
        heights = jnp.exp(jax.random.uniform(jax.random.fold_in(own, dim), (shards_of,), jnp.float32, smallest / len(shards), largest / len(shards)))
        level = level * jnp.repeat(heights, shape[dim] // shards_of).reshape([-1 if axis == dim else 1 for axis in range(len(shape))])
    return level


def centred(own_key, shape, scale, most, cuts=(), kind=jnp.bfloat16):
    values = scale * jax.random.normal(own_key, shape, jnp.float32)
    if cuts:
        values = values * levels(own_key, shape, cuts, -0.22, 0.18)
    return jnp.clip(values, -most, most).astype(kind)


def setup_inputs(seed: int = 0) -> dict:
    arg_keys = jax.random.split(jax.random.key(seed), 12)
    tokens = centred(arg_keys[0], (TOKENS, D), 1.0, 6.0, ((0, 16),))
    cotangent = centred(arg_keys[1], (TOKENS, D), 1.0, 6.0, ((0, 16),))
    norm_gains = jnp.clip(1.0 + 0.1 * jax.random.normal(arg_keys[2], (2, D), jnp.float32), 0.5, 1.5)
    mix_weight = centred(arg_keys[3], (D, 5, HK), D ** -0.5, 0.125, ((0, 16), (2, 2)))
    rate_weight = centred(arg_keys[4], (D, 2, H), D ** -0.5, 0.125, ((0, 16), (2, 2)))
    feed_weight = centred(arg_keys[5], (D, 3, FF), D ** -0.5, 0.125, ((0, 16), (2, 2)))
    conv_weight = jnp.clip(jax.random.uniform(arg_keys[6], (CONV, 3, HK), jnp.float32, -0.8, 0.8) * levels(arg_keys[6], (CONV, 3, HK), ((2, 2),), -0.4, 0.0), -0.8, 0.8)
    decay_log = jnp.clip(2.77 * jax.random.uniform(arg_keys[7], (H,), jnp.float32) ** levels(arg_keys[7], (H,), ((0, 2),), -0.2, 0.2), 0.0, 2.77)
    decay_bias = jnp.clip(-6.9 + 4.6000001430511475 * jax.random.uniform(arg_keys[8], (H,), jnp.float32) ** levels(arg_keys[8], (H,), ((0, 2),), -0.2, 0.2), -6.9, -2.3)
    head_gain = jnp.clip(1.0 + 0.1 * jax.random.normal(arg_keys[9], (H, DK), jnp.float32), 0.5, 1.5)
    doc_starts = draw_doc_starts(jax.random.fold_in(arg_keys[11], 71), 0)
    return dict(tokens=tokens, cotangent=cotangent, norm_gains=norm_gains, mix_weight=mix_weight, rate_weight=rate_weight, feed_weight=feed_weight, conv_weight=conv_weight, decay_log=decay_log, decay_bias=decay_bias, head_gain=head_gain, doc_starts=doc_starts)


precise_mode = lax.Precision.HIGHEST
epsilon = 1e-06
head_epsilon = 0.01

@jax.custom_vjp
def low(v):
    return lax.optimization_barrier(v.astype(jnp.bfloat16)).astype(jnp.float32)

@jax.custom_vjp
def low_back(v):
    return v

def low_keep(v):
    return (low(v), None)

def low_pass(kept, grad):
    return (grad,)

def back_keep(v):
    return (v, None)

def back_low(kept, grad):
    return (low(grad),)
low.defvjp(low_keep, low_pass)
low_back.defvjp(back_keep, back_low)

def norm_rows(value, gain):
    return value * lax.rsqrt(lax.optimization_barrier(jnp.mean(value * value, axis=-1, keepdims=True)) + epsilon) * gain

def head_rows(value, gain):
    return value * lax.rsqrt(lax.optimization_barrier(jnp.mean(value * value, axis=-1, keepdims=True)) + head_epsilon) * gain

def unit_rows(value):
    return value * lax.rsqrt(lax.optimization_barrier(jnp.sum(value * value, axis=-1, keepdims=True)) + epsilon)

def doc_index(positions, starts):
    return (lax.optimization_barrier(jnp.sum((positions[..., None] >= starts).astype(jnp.int32), axis=-1)) - 1).astype(jnp.int32)

def group_step(state_matrix, pieces):
    query_vector, key_vector, value, log_gate, beta, documents, before = pieces
    query_vector = jnp.swapaxes(query_vector, 0, 1)
    key_vector = jnp.swapaxes(key_vector, 0, 1)
    value = jnp.swapaxes(value, 0, 1)
    log_gate = log_gate.T
    beta = beta.T
    length = documents.shape[0]
    places = jnp.arange(length, dtype=jnp.int32)
    same = documents[:, None] == documents[None, :]
    inclusive = same & (places[:, None] >= places[None, :])
    strictly = same & (places[:, None] > places[None, :])
    total = jnp.cumsum(log_gate, axis=1)
    spread = total[:, :, None] - total[:, None, :]
    ratio_in = jnp.where(inclusive, jnp.exp(jnp.where(inclusive, spread, 0.0)), 0.0)
    ratio_strict = jnp.where(strictly, ratio_in, 0.0)
    carried_over = jnp.where((documents == before)[None, :], jnp.exp(total), 0.0)
    key_key = jnp.einsum('hik,hjk->hij', key_vector, key_vector, precision=precise_mode)
    lower = beta[:, :, None] * ratio_strict * key_key
    identity = jnp.eye(length, dtype=lower.dtype)
    known_values = jnp.einsum('jbg,jgn->jbn', key_vector, state_matrix, precision=precise_mode)
    target = beta[:, :, None] * (value - carried_over[:, :, None] * known_values)
    delta_update = lax.linalg.triangular_solve(identity + lower, target, left_side=True, lower=True)
    scores = jnp.einsum('hik,hjk->hij', query_vector, key_vector, precision=precise_mode) * ratio_in
    output_rows = carried_over[:, :, None] * jnp.einsum('jbg,jgn->jbn', query_vector, state_matrix, precision=precise_mode)
    output_rows = output_rows + jnp.einsum('hij,hjv->hiv', scores, delta_update, precision=precise_mode)
    tail_rows = jnp.where((documents == documents[-1])[None, :], jnp.exp(total[:, -1:] - total), 0.0)
    updated_state = carried_over[:, -1, None, None] * state_matrix
    updated_state = updated_state + jnp.einsum('utc,ut,utx->ucx', key_vector, tail_rows, delta_update, precision=precise_mode)
    return (updated_state, jnp.swapaxes(output_rows, 0, 1))

def prepare(padded, rates, taps, decay_log, decay_bias, same):
    count = rates.shape[0]
    reach = taps.shape[0]
    mixed = taps[0] * padded[reach - 1:reach - 1 + count] * same[:, 0, None, None]
    for tap in range(1, reach):
        mixed = mixed + taps[tap] * padded[reach - 1 - tap:reach - 1 - tap + count] * same[:, tap, None, None]
    active = jax.nn.silu(mixed)
    heads = rates.shape[2]
    query_vector = unit_rows(active[:, 0].reshape(count, heads, -1))
    key_vector = unit_rows(active[:, 1].reshape(count, heads, -1))
    value = active[:, 2].reshape(count, heads, -1)
    log_gate = -jnp.exp(decay_log) * jax.nn.softplus(rates[:, 0] + decay_bias)
    beta = jax.nn.sigmoid(rates[:, 1])
    return (query_vector, key_vector, value, log_gate, beta)

def recurrence(query_vector, key_vector, value, log_gate, beta, documents):
    count = query_vector.shape[0] // GROUP
    shaped = lambda array: array.reshape((count, GROUP) + array.shape[1:])
    before = jnp.concatenate([jnp.full((1,), -1, jnp.int32), documents[:-1].astype(jnp.int32)])[::GROUP].astype(jnp.int32)
    state_matrix = jnp.zeros((H, DK, DK), query_vector.dtype)
    final, outputs = lax.scan(jax.checkpoint(group_step), state_matrix, (shaped(query_vector), shaped(key_vector), shaped(value), shaped(log_gate), shaped(beta), shaped(documents), before))
    return outputs.reshape(query_vector.shape)

def block(tokens, norm_gains, mix_weight, rate_weight, feed_weight, conv_weight, decay_log, decay_bias, head_gain, documents, link):
    count = tokens.shape[0]
    normed = low(norm_rows(tokens, norm_gains[0]))
    projected = jnp.einsum('td,dmc->tmc', normed, mix_weight[:, :4], precision=precise_mode)
    pre = low_back(low(projected[:, :3]))
    gate_lin = low_back(projected[:, 3])
    rates = jnp.einsum('td,dmh->tmh', normed, rate_weight, precision=precise_mode)
    padded = jnp.concatenate([jnp.zeros((CONV - 1,) + pre.shape[1:], pre.dtype), pre], 0)
    query_vector, key_vector, value, log_gate, beta = prepare(padded, rates, conv_weight, decay_log, decay_bias, link)
    mixer_out = recurrence(query_vector, key_vector, value, log_gate, beta, documents)
    gated = low(head_rows(mixer_out, head_gain).reshape(count, -1) * jax.nn.silu(gate_lin))
    attended = low_back(jnp.einsum('tc,dc->td', gated, mix_weight[:, 4], precision=precise_mode))
    middle = tokens + attended
    normed2 = low(norm_rows(middle, norm_gains[1]))
    gate_up = low_back(jnp.einsum('td,dmf->tmf', normed2, feed_weight[:, :2], precision=precise_mode))
    hidden = low(jax.nn.silu(gate_up[:, 0]) * gate_up[:, 1])
    branch = low_back(jnp.einsum('tf,df->td', hidden, feed_weight[:, 2], precision=precise_mode))
    return middle + branch

def reference(tokens, cotangent, norm_gains, mix_weight, rate_weight, feed_weight, conv_weight, decay_log, decay_bias, head_gain, doc_starts):
    positions = jnp.arange(TOKENS, dtype=jnp.int32)
    starts = (doc_starts.astype(jnp.int32) + jnp.arange(NSEQS, dtype=jnp.int32)[:, None] * SEQLEN).reshape(-1).astype(jnp.int32)
    documents = doc_index(positions, starts)
    lagged = doc_index(positions[:, None] - jnp.arange(CONV, dtype=jnp.int32)[None, :], starts)
    link = (lagged == documents[:, None]).astype(jnp.float32)
    params = (tokens, norm_gains, mix_weight, rate_weight, feed_weight, conv_weight, decay_log, decay_bias, head_gain)
    params = tuple((item.astype(jnp.float32) for item in params))
    result, pullback = jax.vjp(partial(block, documents=documents, link=link), *params)
    grads = pullback(cotangent.astype(jnp.float32))
    return (result.astype(jnp.bfloat16), grads[0], grads[1], grads[2], grads[3], grads[4], grads[5], grads[6], grads[7], grads[8])
```

```python
from functools import partial

import jax
import jax.numpy as jnp
from jax import lax
from jax.experimental import pallas as pl
from jax.experimental.pallas import tpu as pltpu
from jax.sharding import PartitionSpec as P

f32 = jnp.float32
bf16 = jnp.bfloat16
CHUNK = 128
DK = 128
LANES = 128
HALO = 8
BETA_AT = 16
DOC_AT = 32
epsilon = 1e-06
head_epsilon = 0.01
VMEM_LIMIT = 48 * 1024 * 1024


def mm(a, b):
    return jnp.dot(a, b, preferred_element_type=f32)


def mt(a, b):
    return lax.dot_general(a, b, (((1,), (1,)), ((), ())), preferred_element_type=f32)


def tm(a, b):
    return lax.dot_general(a, b, (((0,), (0,)), ((), ())), preferred_element_type=f32)


def halves(a):
    high = a.astype(bf16)
    return high, (a - high.astype(f32)).astype(bf16)


def mm3(a, b):
    (ah, al), (bh, bl) = a, b
    return mm(ah, bh) + (mm(ah, bl) + mm(al, bh))


def places():
    shape = (CHUNK, CHUNK)
    return lax.broadcasted_iota(jnp.int32, shape, 0), lax.broadcasted_iota(jnp.int32, shape, 1)


def running_sums(cols, rows, at_or_after):
    tril = at_or_after.astype(f32)
    exact = lax.Precision.HIGHEST
    by_col = jnp.dot(tril, cols, precision=exact, preferred_element_type=f32)
    by_row = lax.dot_general(
        rows, tril, (((1,), (1,)), ((), ())), precision=exact, preferred_element_type=f32
    )
    return by_col, by_row


def ratios(by_col, by_row, head, inclusive):
    spread = by_col[:, head : head + 1] - by_row[head : head + 1, :]
    return jnp.exp(jnp.where(inclusive, spread, -1e30))


def entry_and_tail(by_col, cols, head):
    total = by_col[:, head : head + 1]
    entry = jnp.exp(total) * cols[:, DOC_AT + 1 : DOC_AT + 2]
    tail = jnp.exp(total[CHUNK - 1 :, :] - total) * cols[:, DOC_AT + 2 : DOC_AT + 3]
    return entry, tail


def lower_inverse(lowers, row, col):
    eye = (row == col).astype(f32)
    near = (row >> 1) == (col >> 1)
    inverses = [eye - jnp.where(near, low, 0.0) for low in lowers]
    size, shift = 2, 1
    while size < CHUNK:
        block = ((row >> shift) == (col >> shift) + 1) & (((row >> shift) & 1) == 1)
        parts = [halves(jnp.where(block, low, 0.0)) for low in lowers]
        split = [halves(inv) for inv in inverses]
        inner = [halves(mm3(part, inv)) for part, inv in zip(parts, split)]
        inverses = [
            inv - mm3(own, inside) for inv, own, inside in zip(inverses, split, inner)
        ]
        size, shift = size * 2, shift + 1
    return inverses


def lanes(head):
    return slice(head * DK, (head + 1) * DK)


def sigmoid(v):
    return jax.nn.sigmoid(v)


def activate(mixed, width, head):
    raw = [mixed[:, part * width + head * DK : part * width + (head + 1) * DK] for part in range(3)]
    gates = [sigmoid(r) for r in raw]
    active = [r * g for r, g in zip(raw, gates)]
    scales = [
        lax.rsqrt(jnp.sum(a * a, axis=-1, keepdims=True) + epsilon) for a in active[:2]
    ]
    return raw, gates, active, scales


def span_kernel(
    heads, cols_ref, rows_ref, mixed_ref,
    q_ref, k_ref, v_ref, out0_ref, reach_ref, inv_ref, score_ref, w_ref, delta_ref, start_ref,
    final_ref, state_ref,
):
    step = pl.program_id(0)
    row, col = places()
    width = heads * DK

    @pl.when(step == 0)
    def _():
        eye = (row == col).astype(f32)
        for h in range(heads):
            state_ref[h, :, :DK] = jnp.zeros((DK, DK), f32)
            state_ref[h, :, DK:] = eye

    cols, rows = cols_ref[...], rows_ref[...]
    mixed = mixed_ref[...]
    by_col, by_row = running_sums(cols, rows[:8], row >= col)
    same = cols[:, DOC_AT : DOC_AT + 1] == rows[8:9, :]
    inclusive = same & (row >= col)
    strict = row > col
    queries, keys, values, lowers, ratio = [], [], [], [], []
    for h in range(heads):
        _, _, active, scales = activate(mixed, width, h)
        q = (active[0] * scales[0]).astype(bf16)
        k = (active[1] * scales[1]).astype(bf16)
        v = active[2].astype(bf16)
        q_ref[:, lanes(h)] = q
        k_ref[:, lanes(h)] = k
        v_ref[:, lanes(h)] = v
        gamma = ratios(by_col, by_row, h, inclusive)
        beta = cols[:, BETA_AT + h : BETA_AT + h + 1]
        queries.append(q)
        keys.append(k)
        values.append(v)
        ratio.append(gamma)
        lowers.append(jnp.where(strict, beta * gamma * mt(k, k), 0.0))
    inverses = lower_inverse(lowers, row, col)
    for h in range(heads):
        q, k, v = queries[h], keys[h], values[h]
        beta = cols[:, BETA_AT + h : BETA_AT + h + 1]
        entry, tail = entry_and_tail(by_col, cols, h)
        inv = inverses[h].astype(bf16)
        inv_ref[:, lanes(h)] = inv
        score = (mt(q, k) * ratio[h]).astype(bf16)
        score_ref[:, lanes(h)] = score
        target = jnp.concatenate(
            [(v.astype(f32) * beta).astype(bf16), (k.astype(f32) * (beta * entry)).astype(bf16)], 1
        )
        solved = mm(inv, target)
        w = solved[:, DK:].astype(bf16)
        w_ref[:, lanes(h)] = w
        state = state_ref[h]
        state16 = state.astype(bf16)
        start_ref[:, 2 * h * DK : 2 * (h + 1) * DK] = state16
        moved = mm(w, state16)
        delta = jnp.concatenate([solved[:, :DK] - moved[:, :DK], -moved[:, DK:]], 1).astype(bf16)
        delta_ref[:, 2 * h * DK : 2 * (h + 1) * DK] = delta
        out = entry * mm(q, state16) + mm(score, delta)
        out0_ref[:, lanes(h)] = out[:, :DK]
        reach_ref[:, lanes(h)] = out[:, DK:].astype(bf16)
        key_tail = (k.astype(f32) * tail).astype(bf16)
        new = entry[CHUNK - 1 :, :] * state + tm(key_tail, delta)
        state_ref[h] = new
        final_ref[:, 2 * h * DK : 2 * (h + 1) * DK] = new.astype(bf16)


def chunk_spec(width, count=None):
    if count is None:
        return pl.BlockSpec((CHUNK, width), lambda i: (i, 0))
    return pl.BlockSpec((CHUNK, width), lambda i: (count - 1 - i, 0))


def cost(flops, moved):
    return pl.CostEstimate(flops=int(flops), bytes_accessed=int(moved), transcendentals=0)


def run_span(cols, rows, mixed, heads):
    length = mixed.shape[0]
    width = heads * DK
    narrow = jax.ShapeDtypeStruct((length, width), bf16)
    double = jax.ShapeDtypeStruct((length, 2 * width), bf16)
    return pl.pallas_call(
        partial(span_kernel, heads),
        grid=(length // CHUNK,),
        in_specs=[
            chunk_spec(LANES),
            pl.BlockSpec((16, CHUNK), lambda i: (0, i)),
            chunk_spec(3 * width),
        ],
        out_specs=[chunk_spec(width)] * 8
        + [chunk_spec(2 * width)] * 2
        + [pl.BlockSpec((DK, 2 * width), lambda i: (0, 0))],
        out_shape=[
            narrow, narrow, narrow, jax.ShapeDtypeStruct((length, width), f32), narrow, narrow, narrow, narrow,
            double, double, jax.ShapeDtypeStruct((DK, 2 * width), bf16),
        ],
        scratch_shapes=[pltpu.VMEM((heads, DK, 2 * DK), f32)],
        compiler_params=pltpu.CompilerParams(
            dimension_semantics=("arbitrary",), vmem_limit_bytes=VMEM_LIMIT
        ),
        cost_estimate=cost(length * width * 128 * 100, length * width * 30),
        name="span_forward",
    )(cols, rows, mixed)


def enter_kernel(
    heads, place_ref, all_ref, out0_ref, reach_ref, delta_ref, start_ref, gate_ref, gain_ref,
    gated_ref, out_ref, delta_out_ref, state_out_ref, state_ref,
):
    step = pl.program_id(0)

    @pl.when(step == 0)
    def _():
        state_ref[...] = jnp.zeros_like(state_ref)

        def join(turn, carry):
            slot = place_ref[1 + turn]
            for h in range(heads):
                both = all_ref[slot, :, 2 * h * DK : 2 * (h + 1) * DK]
                state = state_ref[:, lanes(h)].astype(bf16)
                state_ref[:, lanes(h)] = mm(both[:, DK:], state) + both[:, :DK].astype(f32)
            return carry

        lax.fori_loop(0, place_ref[0], join, 0)

    for h in range(heads):
        state = state_ref[:, lanes(h)].astype(bf16)
        start = start_ref[:, 2 * h * DK : 2 * (h + 1) * DK]
        delta = delta_ref[:, 2 * h * DK : 2 * (h + 1) * DK]
        state_out_ref[:, lanes(h)] = (mm(start[:, DK:], state) + start[:, :DK].astype(f32)).astype(bf16)
        delta_out_ref[:, lanes(h)] = (mm(delta[:, DK:], state) + delta[:, :DK].astype(f32)).astype(bf16)
        out = out0_ref[:, lanes(h)] + mm(reach_ref[:, lanes(h)], state)
        out_ref[:, lanes(h)] = out
        scale = lax.rsqrt(jnp.mean(out * out, axis=-1, keepdims=True) + head_epsilon)
        gate = gate_ref[:, lanes(h)]
        gated = out * scale * gain_ref[h : h + 1, :] * (gate * sigmoid(gate))
        gated_ref[:, lanes(h)] = gated.astype(bf16)


def run_enter(place, gathered, out0, reach, delta, start, gate_lin, head_gain):
    length, width = out0.shape
    heads = width // DK
    spec = lambda w: pl.BlockSpec((CHUNK, w), lambda i, p: (i, 0))
    narrow = jax.ShapeDtypeStruct((length, width), bf16)
    return pl.pallas_call(
        partial(enter_kernel, heads),
        grid_spec=pltpu.PrefetchScalarGridSpec(
            num_scalar_prefetch=1,
            grid=(length // CHUNK,),
            in_specs=[
                pl.BlockSpec(gathered.shape, lambda i, p: (0, 0, 0)),
                spec(width), spec(width), spec(2 * width), spec(2 * width), spec(width),
                pl.BlockSpec(head_gain.shape, lambda i, p: (0, 0)),
            ],
            out_specs=[spec(width)] * 4,
            scratch_shapes=[pltpu.VMEM((DK, width), f32)],
        ),
        out_shape=[narrow, jax.ShapeDtypeStruct((length, width), f32), narrow, narrow],
        compiler_params=pltpu.CompilerParams(
            dimension_semantics=("arbitrary",), vmem_limit_bytes=VMEM_LIMIT
        ),
        cost_estimate=cost(length * width * 128 * 8, length * width * 24),
        name="span_enter",
    )(place, gathered, out0, reach, delta, start, gate_lin, head_gain)


def back_span_kernel(
    heads, cols_ref, rows_ref, grad_ref, out_ref, gate_ref, gain_ref, q_ref, k_ref, score_ref, w_ref,
    out_grad_ref, gate_grad_ref, gain_grad_ref, final_ref, state_ref,
):
    step = pl.program_id(0)
    row, col = places()

    @pl.when(step == 0)
    def _():
        state_ref[...] = jnp.zeros_like(state_ref)
        gain_grad_ref[...] = jnp.zeros_like(gain_grad_ref)

    cols, rows = cols_ref[...], rows_ref[...]
    by_col, _ = running_sums(cols, rows[:8], row >= col)
    for h in range(heads):
        out, gate, grad = out_ref[:, lanes(h)], gate_ref[:, lanes(h)], grad_ref[:, lanes(h)]
        gain = gain_ref[h : h + 1, :]
        scale = lax.rsqrt(jnp.mean(out * out, axis=-1, keepdims=True) + head_epsilon)
        unit = out * scale
        sig = sigmoid(gate)
        silu = gate * sig
        weighted = grad * unit
        gate_grad_ref[:, lanes(h)] = (
            weighted * gain * (sig * (1.0 + gate * (1.0 - sig)))
        ).astype(bf16)
        gain_grad_ref[h : h + 1, :] += jnp.sum(weighted * silu, axis=0, keepdims=True)
        unit_grad = grad * gain * silu
        out_grad = scale * (unit_grad - unit * jnp.mean(unit_grad * unit, axis=-1, keepdims=True))
        out_grad = out_grad.astype(bf16)
        out_grad_ref[:, lanes(h)] = out_grad
        entry, tail = entry_and_tail(by_col, cols, h)
        state = state_ref[:, lanes(h)]
        key_tail = (k_ref[:, lanes(h)].astype(f32) * tail).astype(bf16)
        query_entry = (q_ref[:, lanes(h)].astype(f32) * entry).astype(bf16)
        delta_grad = tm(score_ref[:, lanes(h)], out_grad) + mm(key_tail, state.astype(bf16))
        new = (
            entry[CHUNK - 1 :, :] * state
            + tm(query_entry, out_grad)
            - tm(w_ref[:, lanes(h)], delta_grad.astype(bf16))
        )
        state_ref[:, lanes(h)] = new
        final_ref[:, lanes(h)] = new.astype(bf16)


def run_back_span(cols, rows, grad, out, gate_lin, head_gain, q, k, score, w):
    length, width = out.shape
    heads = width // DK
    count = length // CHUNK
    spec = chunk_spec(width, count)
    narrow = jax.ShapeDtypeStruct((length, width), bf16)
    fixed = lambda shape: pl.BlockSpec(shape, lambda i: (0, 0))
    return pl.pallas_call(
        partial(back_span_kernel, heads),
        grid=(count,),
        in_specs=[
            chunk_spec(LANES, count),
            pl.BlockSpec((16, CHUNK), lambda i: (0, count - 1 - i)),
            spec, spec, spec, fixed(head_gain.shape), spec, spec, spec, spec,
        ],
        out_specs=[spec, spec, fixed((heads, DK)), fixed((DK, width))],
        out_shape=[
            narrow, narrow, jax.ShapeDtypeStruct((heads, DK), f32), jax.ShapeDtypeStruct((DK, width), bf16),
        ],
        scratch_shapes=[pltpu.VMEM((DK, width), f32)],
        compiler_params=pltpu.CompilerParams(
            dimension_semantics=("arbitrary",), vmem_limit_bytes=VMEM_LIMIT
        ),
        cost_estimate=cost(length * width * 128 * 10, length * width * 24),
        name="back_span",
    )(cols, rows, grad, out, gate_lin, head_gain, q, k, score, w)


def back_kernel(
    heads, chips, place_ref, all_ref, grads_ref, cols_ref, rows_ref, mixed_ref, q_ref, k_ref, v_ref,
    out_grad_ref, inv_ref, score_ref, w_ref, delta_ref, start_ref,
    mixed_grad_ref, col_grad_ref, row_grad_ref, state_ref,
):
    step = pl.program_id(0)
    row, col = places()
    width = heads * DK

    @pl.when(step == 0)
    def _():
        state_ref[...] = jnp.zeros_like(state_ref)

        def join(turn, carry):
            slot = place_ref[chips - turn]
            for h in range(heads):
                move = all_ref[slot, :, (2 * h + 1) * DK : 2 * (h + 1) * DK]
                state = state_ref[:, lanes(h)].astype(bf16)
                state_ref[:, lanes(h)] = tm(move, state) + grads_ref[slot, :, lanes(h)].astype(f32)
            return carry

        lax.fori_loop(0, chips - 1 - place_ref[0], join, 0)

    cols, rows = cols_ref[...], rows_ref[...]
    mixed = mixed_ref[...]
    at_or_after = row >= col
    by_col, by_row = running_sums(cols, rows[:8], at_or_after)
    same = cols[:, DOC_AT : DOC_AT + 1] == rows[8:9, :]
    inclusive = same & at_or_after
    strict = row > col
    lane = lax.broadcasted_iota(jnp.int32, (CHUNK, LANES), 1)
    last = lax.broadcasted_iota(jnp.int32, (CHUNK, 1), 0) == CHUNK - 1
    sub = lax.broadcasted_iota(jnp.int32, (8, CHUNK), 0)
    gate_cols = jnp.zeros((CHUNK, LANES), f32)
    beta_cols = jnp.zeros((CHUNK, LANES), f32)
    gate_rows = jnp.zeros((8, CHUNK), f32)
    rowsum = lambda a: jnp.sum(a, axis=-1, keepdims=True)
    for h in range(heads):
        q, k, v = q_ref[:, lanes(h)], k_ref[:, lanes(h)], v_ref[:, lanes(h)]
        q32, k32, v32 = q.astype(f32), k.astype(f32), v.astype(f32)
        out_grad, inv, score = out_grad_ref[:, lanes(h)], inv_ref[:, lanes(h)], score_ref[:, lanes(h)]
        w, delta, start = w_ref[:, lanes(h)], delta_ref[:, lanes(h)], start_ref[:, lanes(h)]
        beta = cols[:, BETA_AT + h : BETA_AT + h + 1]
        entry, tail = entry_and_tail(by_col, cols, h)
        gamma = ratios(by_col, by_row, h, inclusive)
        lower = jnp.where(strict, gamma * mt(k, k), 0.0)
        state = state_ref[:, lanes(h)]
        state16 = state.astype(bf16)
        key_tail = (k32 * tail).astype(bf16)
        query_entry = (q32 * entry).astype(bf16)
        delta_grad = (tm(score, out_grad) + mm(key_tail, state16)).astype(bf16)
        target_grad = tm(inv, delta_grad)
        target_grad16 = target_grad.astype(bf16)
        score_grad = mt(out_grad, delta)
        lower_grad = -mt(target_grad16, delta)
        out_state = mt(out_grad, start)
        target_state = mt(target_grad16, start)
        tail_grad = mt(delta, state16)
        score_part = (score_grad * gamma).astype(bf16)
        scaled = jnp.where(strict, lower_grad * gamma * beta, 0.0).astype(bf16)
        q_grad = entry * out_state + mm(score_part, k)
        k_grad = (
            tm(score_part, q) + tail * tail_grad - (beta * entry) * target_state
            + mm(scaled, k) + tm(scaled, k)
        )
        v_grad = beta * target_grad
        state_ref[:, lanes(h)] = (
            entry[CHUNK - 1 :, :] * state + tm(query_entry, out_grad) - tm(w, delta_grad)
        )
        lower_part = lower_grad * lower
        through = score_grad * score.astype(f32) + beta * lower_part
        entry_part = rowsum(target_state * k32) * entry
        tail_part = rowsum(tail_grad * k32) * tail
        carried = jnp.sum(rowsum(start.astype(f32) * state), axis=0, keepdims=True)
        at_end = jnp.sum(tail_part, axis=0, keepdims=True) + entry[CHUNK - 1 :, :] * carried
        gate_col = rowsum(through) + entry * rowsum(out_state * q32) - beta * entry_part - tail_part
        gate_col = gate_col + jnp.where(last, at_end, 0.0)
        beta_col = rowsum(target_grad * v32) - entry_part + rowsum(lower_part)
        gate_cols = jnp.where(lane == h, gate_col, gate_cols)
        beta_cols = jnp.where(lane == BETA_AT + h, beta_col, beta_cols)
        gate_rows = jnp.where(sub == h, jnp.sum(through, axis=0, keepdims=True), gate_rows)
        raw, gates, active, scales = activate(mixed, width, h)
        grads = []
        for part, grad in enumerate((q_grad, k_grad)):
            unit = active[part] * scales[part]
            grads.append(scales[part] * (grad - unit * rowsum(grad * unit)))
        grads.append(v_grad)
        for part in range(3):
            slope = gates[part] * (1.0 + raw[part] * (1.0 - gates[part]))
            at = part * width + h * DK
            mixed_grad_ref[:, at : at + DK] = grads[part] * slope
    exact = lax.Precision.HIGHEST
    tril = at_or_after.astype(f32)
    summed = lax.dot_general(
        tril, gate_cols, (((0,), (0,)), ((), ())), precision=exact, preferred_element_type=f32
    )
    col_grad_ref[...] = summed + beta_cols
    row_grad_ref[...] = jnp.dot(gate_rows, tril, precision=exact, preferred_element_type=f32)


def run_back(place, gathered, grads, cols, rows, mixed, q, k, v, out_grad, inv, score, w, delta, start):
    length, width = q.shape
    heads = width // DK
    count = length // CHUNK
    spec = lambda w: pl.BlockSpec((CHUNK, w), lambda i, p: (count - 1 - i, 0))
    whole = lambda shape: pl.BlockSpec(shape, lambda i, p: (0, 0, 0))
    return pl.pallas_call(
        partial(back_kernel, heads, gathered.shape[0]),
        grid_spec=pltpu.PrefetchScalarGridSpec(
            num_scalar_prefetch=1,
            grid=(count,),
            in_specs=[
                whole(gathered.shape), whole(grads.shape), spec(LANES),
                pl.BlockSpec((16, CHUNK), lambda i, p: (0, count - 1 - i)),
                spec(3 * width),
            ] + [spec(width)] * 9,
            out_specs=[
                spec(3 * width), spec(LANES), pl.BlockSpec((8, CHUNK), lambda i, p: (0, count - 1 - i)),
            ],
            scratch_shapes=[pltpu.VMEM((DK, width), f32)],
        ),
        out_shape=[
            jax.ShapeDtypeStruct((length, 3 * width), f32),
            jax.ShapeDtypeStruct((length, LANES), f32),
            jax.ShapeDtypeStruct((8, length), f32),
        ],
        compiler_params=pltpu.CompilerParams(
            dimension_semantics=("arbitrary",), vmem_limit_bytes=VMEM_LIMIT
        ),
        cost_estimate=cost(length * width * 128 * 36, length * width * 40),
        name="span_backward",
    )(place, gathered, grads, cols, rows, mixed, q, k, v, out_grad, inv, score, w, delta, start)


def norm_rows(value, gain):
    return value * lax.rsqrt(jnp.mean(value * value, axis=-1, keepdims=True) + epsilon) * gain


def doc_index(positions, starts):
    return jnp.sum((positions[..., None] >= starts).astype(jnp.int32), axis=-1) - 1


def swish_product(gate, up):
    return jax.nn.silu(gate) * up


def dot(a, b):
    return jnp.dot(a, b, preferred_element_type=f32)


def dot_t(a, b):
    return lax.dot_general(a, b, (((1,), (1,)), ((), ())), preferred_element_type=f32)


def ring_of(chips):
    rows = max(1, chips // 4)
    if rows < 2 or chips % rows:
        return list(range(chips))
    depth = chips // rows
    order = [z * rows for z in range(depth)]
    for z in range(depth - 1, -1, -1):
        line = [z * rows + y for y in range(1, rows)]
        order += line if (depth - 1 - z) % 2 == 0 else line[::-1]
    return order


def shards(
    tokens, cotangent, norm_gains, mix_weight, rate_weight, feed_weight, conv_weight,
    decay_log, decay_bias, head_gain, doc_starts,
):
    count, model = tokens.shape
    spans = lax.axis_size("seq")
    chips = spans // 2
    tensors = lax.axis_size("tensor")
    place = lax.axis_index("seq")
    core = lax.rem(place, 2)
    chip = lax.div(place, 2)
    first_core = core == 0
    rows = mix_weight.shape[0]
    heads_all = decay_log.shape[0]
    heads = heads_all // 2
    width = heads * DK
    hidden_width = feed_weight.shape[2] // 2
    length = 2 * count
    reach = conv_weight.shape[0]
    ring = ring_of(chips)
    ring_place = [ring.index(c) for c in range(chips)]
    my_ring = jnp.asarray(ring_place, jnp.int32)[chip]

    def core_swap(a):
        return lax.ppermute(a, "seq", [(i, i ^ 1) for i in range(spans)])

    def ring_shift(a, by):
        pairs = [
            (2 * ring[i] + k, 2 * ring[(i + by) % chips] + k) for i in range(chips) for k in range(2)
        ]
        return lax.ppermute(a, "seq", pairs)

    def tensor_sum(a):
        a = a.astype(bf16)
        if tensors == 2:
            return a.astype(f32) + lax.ppermute(a, "tensor", [(0, 1), (1, 0)]).astype(f32)
        return lax.psum(a, "tensor").astype(f32)

    def ring_gather(a):
        held = [a] + [None] * (chips - 1)
        up = down = a
        for hop in range(1, chips // 2 + 1):
            up = ring_shift(up, 1)
            held[hop] = up
            if hop < chips - hop:
                down = ring_shift(down, -1)
                held[chips - hop] = down
        return jnp.stack(held)

    def mine_first(a):
        return jnp.where(first_core, a, jnp.concatenate([a[count:], a[:count]], 0))

    def pair_sum(a, weight):
        theirs = lax.dynamic_slice_in_dim(a, (1 - core) * count, count, 0)
        own = lax.dynamic_slice_in_dim(a, core * count, count, 0)
        arrived = core_swap(dot_t(theirs, weight).astype(bf16))
        return tensor_sum(dot_t(own, weight) + arrived.astype(f32))

    def in_order(own, other):
        return jnp.where(
            first_core, jnp.concatenate([own, other], 0), jnp.concatenate([other, own], 0)
        )

    def gather(parts):
        packed = jnp.concatenate([p.reshape(rows, 2, -1).swapaxes(0, 1) for p in parts], 2)
        everything = lax.all_gather(packed, "seq", axis=1, tiled=True)
        return lax.dynamic_index_in_dim(everything, core, 0, False)

    rate_parts = rate_weight.reshape(rows, 2, 2, heads).swapaxes(1, 2).reshape(rows, 2, 2 * heads)
    rate_parts = jnp.pad(rate_parts, ((0, 0), (0, 0), (0, LANES - 2 * heads)))
    mix_parts = [mix_weight[:, m] for m in range(5)]
    feed_parts = [feed_weight[:, m] for m in range(3)]
    qkv_weight = gather(mix_parts[:3] + [rate_parts])
    gate_out = gather(mix_parts[3:])
    gate_weight, out_weight = gate_out[:, :width], gate_out[:, width:]
    pair_weight = gather(feed_parts[:2])
    down_weight = gather(feed_parts[2:])

    seq_count = doc_starts.shape[0]
    seq_len = count * spans // seq_count
    starts = (doc_starts + jnp.arange(seq_count, dtype=jnp.int32)[:, None] * seq_len).reshape(-1)
    positions = chip * length + jnp.arange(length, dtype=jnp.int32)
    documents = doc_index(positions, starts)
    lagged = doc_index(positions[:, None] - jnp.arange(reach, dtype=jnp.int32)[None, :], starts)
    link = (lagged == documents[:, None]).astype(f32)
    by_chunk = documents.reshape(-1, CHUNK)
    before = doc_index(positions[::CHUNK] - 1, starts)
    carry = (by_chunk == before[:, None]).astype(f32).reshape(length)
    tail = (by_chunk == by_chunk[:, -1:]).astype(f32).reshape(length)

    inputs = tokens.astype(f32)
    other_tokens = core_swap(tokens)
    cot_other = core_swap(cotangent)
    edge = tokens[count - HALO :]
    halo = lax.ppermute(edge, "seq", [(2 * c + 1, 2 * c + 2) for c in range(chips - 1)])
    halo = halo + lax.ppermute(edge, "seq", [(2 * c + 1, 2 * c + 3) for c in range(chips - 1)])
    _, norm_first_back = jax.vjp(norm_rows, inputs, norm_gains[0])
    chip_tokens = jnp.concatenate([halo, in_order(tokens, other_tokens)], 0).astype(f32)
    normed_halo = norm_rows(chip_tokens, norm_gains[0]).astype(bf16)
    normed = normed_halo[HALO:]

    projected = dot(normed_halo, qkv_weight)
    padded = projected[:, : 3 * width].astype(bf16).astype(f32)
    rates = projected[HALO:, 3 * width : 3 * width + 2 * heads]
    gate_lin = dot(normed, gate_weight)
    own_taps = lax.dynamic_slice_in_dim(
        conv_weight.reshape(reach, 3, 2, width), core, 1, 2
    ).reshape(reach, 3 * width)
    own = lambda a: lax.dynamic_slice_in_dim(a, core * heads, heads, 0)
    log_scale, bias, gain = own(decay_log), own(decay_bias), own(head_gain)

    def convolve(padded, taps):
        mixed = taps[0] * padded[HALO:] * link[:, 0:1]
        for tap in range(1, reach):
            mixed = mixed + taps[tap] * padded[HALO - tap : HALO - tap + length] * link[:, tap : tap + 1]
        return mixed

    def gates(rates, log_scale, bias):
        log_gate = -jnp.exp(log_scale) * jax.nn.softplus(rates[:, :heads] + bias)
        return log_gate, jax.nn.sigmoid(rates[:, heads:])

    mixed, convolve_back = jax.vjp(convolve, padded, own_taps)
    (log_gate, beta), gates_back = jax.vjp(gates, rates, log_scale, bias)
    doc_parts = jnp.stack([documents.astype(f32), carry, tail], 1)
    cols = jnp.concatenate(
        [
            jnp.pad(log_gate, ((0, 0), (0, BETA_AT - heads))),
            jnp.pad(beta, ((0, 0), (0, DOC_AT - BETA_AT - heads))),
            jnp.pad(doc_parts, ((0, 0), (0, LANES - DOC_AT - 3))),
        ],
        1,
    )
    by_rows = jnp.concatenate(
        [jnp.pad(log_gate.T, ((0, 8 - heads), (0, 0))), jnp.broadcast_to(documents.astype(f32), (8, length))],
        0,
    )
    q, k, v, out0, reached, inverse, score, w, delta2, start2, final = run_span(cols, by_rows, mixed, heads)
    slots = lax.rem(my_ring - jnp.asarray(ring_place, jnp.int32) + chips, chips)
    place_table = jnp.concatenate([chip[None], slots]).astype(jnp.int32)
    gathered = ring_gather(final)
    gated, mixer_out, delta, start = run_enter(
        place_table, gathered, out0, reached, delta2, start2, gate_lin, gain
    )
    middle = inputs + pair_sum(gated, out_weight)
    normed2_own32, norm_second_back = jax.vjp(norm_rows, middle, norm_gains[1])
    normed2_own = normed2_own32.astype(bf16)

    normed2 = jnp.concatenate([normed2_own, core_swap(normed2_own)], 0)
    cot = jnp.concatenate([cotangent, cot_other], 0)
    gate_up = dot(normed2, pair_weight)
    hidden32, swish_back = jax.vjp(swish_product, gate_up[:, :hidden_width], gate_up[:, hidden_width:])
    hidden = hidden32.astype(bf16)
    hidden_grad = dot(cot, down_weight)
    pair_grad = jnp.concatenate([g.astype(bf16) for g in swish_back(hidden_grad)], 1)

    def halves_sum(a, weight):
        arrived = core_swap(dot_t(a[count:], weight).astype(bf16))
        return tensor_sum(dot_t(a[:count], weight) + arrived.astype(f32))

    second_grad = halves_sum(pair_grad, pair_weight)
    block_out = (middle + halves_sum(hidden, down_weight)).astype(bf16)

    def ring_reduce(left, right):
        done = []
        for way, half in ((1, core), (-1, 1 - core)):
            total = None
            for step in range(chips):
                owner = jnp.asarray(ring, jnp.int32)[lax.rem(my_ring - way * (1 + step) + 2 * chips, chips)]
                part = lax.dynamic_slice_in_dim(left, owner * 2 * rows + half * rows, rows, 1)
                term = lax.dot_general(part, right, (((0,), (0,)), ((), ())), preferred_element_type=f32)
                if total is not None:
                    term = term + total.astype(f32)
                if step < chips - 1:
                    total = ring_shift(term.astype(bf16), way)
            done.append(term)
        return done[0], core_swap(done[1].astype(bf16)).astype(f32)

    down_sum = ring_reduce(cot, hidden)
    pair_sums = ring_reduce(normed2, pair_grad)

    middle_norm_grad, gain_second_grad = norm_second_back(second_grad)
    middle_grad = cotangent.astype(f32) + middle_norm_grad
    attended_grad_own = middle_grad.astype(bf16)
    attended_grad = in_order(attended_grad_own, core_swap(attended_grad_own))
    out_sum = ring_reduce(attended_grad, gated)
    gated_grad = dot(attended_grad, out_weight)
    out_grad, gate_lin_grad, head_gain_grad, local_grad = run_back_span(
        cols, by_rows, gated_grad, mixer_out, gate_lin, gain, q, k, score, w
    )
    state_grads = ring_gather(local_grad)
    mixed_grad, col_grads, row_grads = run_back(
        place_table, gathered, state_grads, cols, by_rows, mixed, q, k, v, out_grad, inverse, score, w, delta, start
    )
    log_gate_grad = col_grads[:, :heads] - row_grads[:heads].T
    beta_grad = col_grads[:, BETA_AT : BETA_AT + heads]
    rates_grad, log_scale_grad, bias_grad = gates_back((log_gate_grad, beta_grad))
    padded_grad, taps_grad = convolve_back(mixed_grad)
    returned = lax.ppermute(
        padded_grad[:HALO],
        "seq",
        [(2 * c + k, 2 * c - 2 + k) for c in range(1, chips) for k in range(2)],
    )
    pre_grad = padded_grad[HALO:].at[length - HALO :].add(returned)
    projected_grad = jnp.concatenate([pre_grad.astype(bf16), gate_lin_grad], 1)
    rates_grad16 = jnp.pad(rates_grad, ((0, 0), (0, LANES - 2 * heads))).astype(bf16)
    first_left = jnp.concatenate([projected_grad[:, : 3 * width], rates_grad16, gate_lin_grad], 1)
    first_weight = jnp.concatenate([qkv_weight, gate_weight], 1)
    first_grad = pair_sum(first_left, first_weight)
    token_norm_grad, gain_first_grad = norm_first_back(first_grad)
    token_gradient = middle_grad + token_norm_grad
    mix_sum = ring_reduce(normed, projected_grad)
    rate_sum = lax.dot_general(
        rates_grad, normed.astype(f32), (((0,), (0,)), ((), ())), precision=lax.Precision.HIGHEST
    )

    def both_halves(own, other):
        return jnp.where(first_core, jnp.concatenate([own, other], 2), jnp.concatenate([other, own], 2))

    shape = lambda a, parts: a.reshape(rows, parts, -1)
    mix_gradient = both_halves(
        *[
            jnp.concatenate([shape(a, 4), shape(b, 1)], 1) for a, b in zip(mix_sum, out_sum)
        ]
    )
    feed_gradient = both_halves(
        *[jnp.concatenate([shape(a, 2), shape(b, 1)], 1) for a, b in zip(pair_sums, down_sum)]
    )

    def widen(a, axis):
        nothing = jnp.zeros_like(a)
        return jnp.where(
            first_core, jnp.concatenate([a, nothing], axis), jnp.concatenate([nothing, a], axis)
        )

    small = [
        jnp.stack([gain_first_grad, gain_second_grad]),
        widen(taps_grad.reshape(reach, 3, width), 2),
        widen(log_scale_grad, 0),
        widen(bias_grad, 0),
        widen(head_gain_grad, 0),
        widen(rate_sum.reshape(2, heads, model), 1),
    ]
    flat = lax.psum(jnp.concatenate([a.reshape(-1) for a in small]), "seq")
    summed, at = [], 0
    for a in small:
        summed.append(flat[at : at + a.size].reshape(a.shape))
        at += a.size
    rate_gradient = lax.dynamic_slice_in_dim(summed[5], place * rows, rows, 2).transpose(2, 0, 1)
    return (
        block_out, token_gradient, summed[0], mix_gradient, rate_gradient, feed_gradient,
        summed[1], summed[2], summed[3], summed[4],
    )


def solution(mesh):
    return jax.shard_map(
        shards,
        mesh=mesh,
        in_specs=(
            P("seq", None),
            P("seq", None),
            P(),
            P("seq", None, "tensor"),
            P("seq", None, "tensor"),
            P("seq", None, "tensor"),
            P(None, None, "tensor"),
            P("tensor"),
            P("tensor"),
            P("tensor", None),
            P(),
        ),
        out_specs=(
            P("seq", None),
            P("seq", None),
            P(),
            P("seq", None, "tensor"),
            P("seq", None, "tensor"),
            P("seq", None, "tensor"),
            P(None, None, "tensor"),
            P("tensor"),
            P("tensor"),
            P("tensor", None),
        ),
        check_vma=False,
    )
```

```python
from functools import partial

import jax
import jax.numpy as jnp
from jax import lax
from jax.experimental import pallas as pl
from jax.experimental.pallas import tpu as pltpu
from jax.sharding import PartitionSpec as P

f32 = jnp.float32
bf16 = jnp.bfloat16
CHUNK = 128
DK = 128
LANES = 128
HALO = 8
BETA_AT = 16
DOC_AT = 32
CORE_AT, OTHER_AT, ZERO_AT, ONE_AT, CHIP_AT, RING_AT = 0, 1, 2, 3, 4, 5
epsilon = 1e-06
head_epsilon = 0.01
VMEM_LIMIT = 48 * 1024 * 1024


def mm(a, b):
    return jnp.dot(a, b, preferred_element_type=f32)


def mt(a, b):
    return lax.dot_general(a, b, (((1,), (1,)), ((), ())), preferred_element_type=f32)


def tm(a, b):
    return lax.dot_general(a, b, (((0,), (0,)), ((), ())), preferred_element_type=f32)


def halves(a):
    high = a.astype(bf16)
    return high, (a - high.astype(f32)).astype(bf16)


def mm3(a, b):
    (ah, al), (bh, bl) = a, b
    return mm(ah, bh) + (mm(ah, bl) + mm(al, bh))


def places():
    shape = (CHUNK, CHUNK)
    return lax.broadcasted_iota(jnp.int32, shape, 0), lax.broadcasted_iota(jnp.int32, shape, 1)


def running_sums(cols, rows, at_or_after):
    tril = at_or_after.astype(f32)
    exact = lax.Precision.HIGHEST
    by_col = jnp.dot(tril, cols, precision=exact, preferred_element_type=f32)
    by_row = lax.dot_general(
        rows, tril, (((1,), (1,)), ((), ())), precision=exact, preferred_element_type=f32
    )
    return by_col, by_row


def ratios(by_col, by_row, head, inclusive):
    spread = by_col[:, head : head + 1] - by_row[head : head + 1, :]
    return jnp.exp(jnp.where(inclusive, spread, -1e30))


def entry_and_tail(by_col, cols, head):
    total = by_col[:, head : head + 1]
    entry = jnp.exp(total) * cols[:, DOC_AT + 1 : DOC_AT + 2]
    tail = jnp.exp(total[CHUNK - 1 :, :] - total) * cols[:, DOC_AT + 2 : DOC_AT + 3]
    return entry, tail


def lower_inverse(lowers, row, col):
    eye = (row == col).astype(f32)
    near = (row >> 1) == (col >> 1)
    inverses = [eye - jnp.where(near, low, 0.0) for low in lowers]
    size, shift = 2, 1
    while size < CHUNK:
        block = ((row >> shift) == (col >> shift) + 1) & (((row >> shift) & 1) == 1)
        parts = [halves(jnp.where(block, low, 0.0)) for low in lowers]
        split = [halves(inv) for inv in inverses]
        inner = [halves(mm3(part, inv)) for part, inv in zip(parts, split)]
        inverses = [
            inv - mm3(own, inside) for inv, own, inside in zip(inverses, split, inner)
        ]
        size, shift = size * 2, shift + 1
    return inverses


def lanes(head):
    return slice(head * DK, (head + 1) * DK)


def sigmoid(v):
    return jax.nn.sigmoid(v)


def activate(mixed, width, head):
    raw = [mixed[:, part * width + head * DK : part * width + (head + 1) * DK] for part in range(3)]
    gates = [sigmoid(r) for r in raw]
    active = [r * g for r, g in zip(raw, gates)]
    scales = [
        lax.rsqrt(jnp.sum(a * a, axis=-1, keepdims=True) + epsilon) for a in active[:2]
    ]
    return raw, gates, active, scales


def span_kernel(
    heads, cols_ref, rows_ref, mixed_ref,
    q_ref, k_ref, v_ref, out0_ref, reach_ref, inv_ref, score_ref, w_ref, delta_ref, start_ref,
    final_ref, state_ref,
):
    step = pl.program_id(0)
    row, col = places()
    width = heads * DK

    @pl.when(step == 0)
    def _():
        eye = (row == col).astype(f32)
        for h in range(heads):
            state_ref[h, :, :DK] = jnp.zeros((DK, DK), f32)
            state_ref[h, :, DK:] = eye

    cols, rows = cols_ref[...], rows_ref[...]
    mixed = mixed_ref[...]
    by_col, by_row = running_sums(cols, rows[:8], row >= col)
    same = cols[:, DOC_AT : DOC_AT + 1] == rows[8:9, :]
    inclusive = same & (row >= col)
    strict = row > col
    queries, keys, values, lowers, ratio = [], [], [], [], []
    for h in range(heads):
        _, _, active, scales = activate(mixed, width, h)
        q = (active[0] * scales[0]).astype(bf16)
        k = (active[1] * scales[1]).astype(bf16)
        v = active[2].astype(bf16)
        q_ref[:, lanes(h)] = q
        k_ref[:, lanes(h)] = k
        v_ref[:, lanes(h)] = v
        gamma = ratios(by_col, by_row, h, inclusive)
        beta = cols[:, BETA_AT + h : BETA_AT + h + 1]
        queries.append(q)
        keys.append(k)
        values.append(v)
        ratio.append(gamma)
        lowers.append(jnp.where(strict, beta * gamma * mt(k, k), 0.0))
    inverses = lower_inverse(lowers, row, col)
    for h in range(heads):
        q, k, v = queries[h], keys[h], values[h]
        beta = cols[:, BETA_AT + h : BETA_AT + h + 1]
        entry, tail = entry_and_tail(by_col, cols, h)
        inv = inverses[h].astype(bf16)
        inv_ref[:, lanes(h)] = inv
        score = (mt(q, k) * ratio[h]).astype(bf16)
        score_ref[:, lanes(h)] = score
        target = jnp.concatenate(
            [(v.astype(f32) * beta).astype(bf16), (k.astype(f32) * (beta * entry)).astype(bf16)], 1
        )
        solved = mm(inv, target)
        w = solved[:, DK:].astype(bf16)
        w_ref[:, lanes(h)] = w
        state = state_ref[h]
        state16 = state.astype(bf16)
        start_ref[:, 2 * h * DK : 2 * (h + 1) * DK] = state16
        moved = mm(w, state16)
        delta = jnp.concatenate([solved[:, :DK] - moved[:, :DK], -moved[:, DK:]], 1).astype(bf16)
        delta_ref[:, 2 * h * DK : 2 * (h + 1) * DK] = delta
        out = entry * mm(q, state16) + mm(score, delta)
        out0_ref[:, lanes(h)] = out[:, :DK]
        reach_ref[:, lanes(h)] = out[:, DK:].astype(bf16)
        key_tail = (k.astype(f32) * tail).astype(bf16)
        new = entry[CHUNK - 1 :, :] * state + tm(key_tail, delta)
        state_ref[h] = new
        final_ref[:, 2 * h * DK : 2 * (h + 1) * DK] = new.astype(bf16)


def chunk_spec(width, count=None):
    if count is None:
        return pl.BlockSpec((CHUNK, width), lambda i: (i, 0))
    return pl.BlockSpec((CHUNK, width), lambda i: (count - 1 - i, 0))


def cost(flops, moved):
    return pl.CostEstimate(flops=int(flops), bytes_accessed=int(moved), transcendentals=0)


def run_span(cols, rows, mixed, heads):
    length = mixed.shape[0]
    width = heads * DK
    narrow = jax.ShapeDtypeStruct((length, width), bf16)
    double = jax.ShapeDtypeStruct((length, 2 * width), bf16)
    return pl.pallas_call(
        partial(span_kernel, heads),
        grid=(length // CHUNK,),
        in_specs=[
            chunk_spec(LANES),
            pl.BlockSpec((16, CHUNK), lambda i: (0, i)),
            chunk_spec(3 * width),
        ],
        out_specs=[chunk_spec(width)] * 8
        + [chunk_spec(2 * width)] * 2
        + [pl.BlockSpec((DK, 2 * width), lambda i: (0, 0))],
        out_shape=[
            narrow, narrow, narrow, jax.ShapeDtypeStruct((length, width), f32), narrow, narrow, narrow, narrow,
            double, double, jax.ShapeDtypeStruct((DK, 2 * width), bf16),
        ],
        scratch_shapes=[pltpu.VMEM((heads, DK, 2 * DK), f32)],
        compiler_params=pltpu.CompilerParams(
            dimension_semantics=("arbitrary",), vmem_limit_bytes=VMEM_LIMIT
        ),
        cost_estimate=cost(length * width * 128 * 100, length * width * 30),
        name="span_forward",
    )(cols, rows, mixed)


def enter_kernel(
    heads, chips, place_ref, all_ref, out0_ref, reach_ref, delta_ref, start_ref, gate_ref, gain_ref,
    gated_ref, out_ref, delta_out_ref, state_out_ref, state_ref,
):
    step = pl.program_id(0)

    @pl.when(step == 0)
    def _():
        state_ref[...] = jnp.zeros_like(state_ref)

        def join(turn, carry):
            slot = place_ref[RING_AT + 2 * chips + turn]
            for h in range(heads):
                both = all_ref[slot, :, 2 * h * DK : 2 * (h + 1) * DK]
                state = state_ref[:, lanes(h)].astype(bf16)
                state_ref[:, lanes(h)] = mm(both[:, DK:], state) + both[:, :DK].astype(f32)
            return carry

        lax.fori_loop(0, place_ref[CHIP_AT], join, 0)

    for h in range(heads):
        state = state_ref[:, lanes(h)].astype(bf16)
        start = start_ref[:, 2 * h * DK : 2 * (h + 1) * DK]
        delta = delta_ref[:, 2 * h * DK : 2 * (h + 1) * DK]
        state_out_ref[:, lanes(h)] = (mm(start[:, DK:], state) + start[:, :DK].astype(f32)).astype(bf16)
        delta_out_ref[:, lanes(h)] = (mm(delta[:, DK:], state) + delta[:, :DK].astype(f32)).astype(bf16)
        out = out0_ref[:, lanes(h)] + mm(reach_ref[:, lanes(h)], state)
        out_ref[:, lanes(h)] = out
        scale = lax.rsqrt(jnp.mean(out * out, axis=-1, keepdims=True) + head_epsilon)
        gate = gate_ref[:, lanes(h)]
        gated = out * scale * gain_ref[h : h + 1, :] * (gate * sigmoid(gate))
        gated_ref[:, lanes(h)] = gated.astype(bf16)


def run_enter(place, gathered, out0, reach, delta, start, gate_lin, head_gain):
    length, width = out0.shape
    heads = width // DK
    spec = lambda w: pl.BlockSpec((CHUNK, w), lambda i, p: (i, 0))
    narrow = jax.ShapeDtypeStruct((length, width), bf16)
    return pl.pallas_call(
        partial(enter_kernel, heads, gathered.shape[0]),
        grid_spec=pltpu.PrefetchScalarGridSpec(
            num_scalar_prefetch=1,
            grid=(length // CHUNK,),
            in_specs=[
                pl.BlockSpec(gathered.shape, lambda i, p: (0, 0, 0)),
                spec(width), spec(width), spec(2 * width), spec(2 * width), spec(width),
                pl.BlockSpec(head_gain.shape, lambda i, p: (0, 0)),
            ],
            out_specs=[spec(width)] * 4,
            scratch_shapes=[pltpu.VMEM((DK, width), f32)],
        ),
        out_shape=[narrow, jax.ShapeDtypeStruct((length, width), f32), narrow, narrow],
        compiler_params=pltpu.CompilerParams(
            dimension_semantics=("arbitrary",), vmem_limit_bytes=VMEM_LIMIT
        ),
        cost_estimate=cost(length * width * 128 * 8, length * width * 24),
        name="span_enter",
    )(place, gathered, out0, reach, delta, start, gate_lin, head_gain)


def back_span_kernel(
    heads, cols_ref, rows_ref, grad_ref, out_ref, gate_ref, gain_ref, q_ref, k_ref, score_ref, w_ref,
    out_grad_ref, gate_grad_ref, gain_grad_ref, final_ref, state_ref,
):
    step = pl.program_id(0)
    row, col = places()

    @pl.when(step == 0)
    def _():
        state_ref[...] = jnp.zeros_like(state_ref)
        gain_grad_ref[...] = jnp.zeros_like(gain_grad_ref)

    cols, rows = cols_ref[...], rows_ref[...]
    by_col, _ = running_sums(cols, rows[:8], row >= col)
    for h in range(heads):
        out, gate, grad = out_ref[:, lanes(h)], gate_ref[:, lanes(h)], grad_ref[:, lanes(h)]
        gain = gain_ref[h : h + 1, :]
        scale = lax.rsqrt(jnp.mean(out * out, axis=-1, keepdims=True) + head_epsilon)
        unit = out * scale
        sig = sigmoid(gate)
        silu = gate * sig
        weighted = grad * unit
        gate_grad_ref[:, lanes(h)] = (
            weighted * gain * (sig * (1.0 + gate * (1.0 - sig)))
        ).astype(bf16)
        gain_grad_ref[h : h + 1, :] += jnp.sum(weighted * silu, axis=0, keepdims=True)
        unit_grad = grad * gain * silu
        out_grad = scale * (unit_grad - unit * jnp.mean(unit_grad * unit, axis=-1, keepdims=True))
        out_grad = out_grad.astype(bf16)
        out_grad_ref[:, lanes(h)] = out_grad
        entry, tail = entry_and_tail(by_col, cols, h)
        state = state_ref[:, lanes(h)]
        key_tail = (k_ref[:, lanes(h)].astype(f32) * tail).astype(bf16)
        query_entry = (q_ref[:, lanes(h)].astype(f32) * entry).astype(bf16)
        delta_grad = tm(score_ref[:, lanes(h)], out_grad) + mm(key_tail, state.astype(bf16))
        new = (
            entry[CHUNK - 1 :, :] * state
            + tm(query_entry, out_grad)
            - tm(w_ref[:, lanes(h)], delta_grad.astype(bf16))
        )
        state_ref[:, lanes(h)] = new
        final_ref[:, lanes(h)] = new.astype(bf16)


def run_back_span(cols, rows, grad, out, gate_lin, head_gain, q, k, score, w):
    length, width = out.shape
    heads = width // DK
    count = length // CHUNK
    spec = chunk_spec(width, count)
    narrow = jax.ShapeDtypeStruct((length, width), bf16)
    fixed = lambda shape: pl.BlockSpec(shape, lambda i: (0, 0))
    return pl.pallas_call(
        partial(back_span_kernel, heads),
        grid=(count,),
        in_specs=[
            chunk_spec(LANES, count),
            pl.BlockSpec((16, CHUNK), lambda i: (0, count - 1 - i)),
            spec, spec, spec, fixed(head_gain.shape), spec, spec, spec, spec,
        ],
        out_specs=[spec, spec, fixed((heads, DK)), fixed((DK, width))],
        out_shape=[
            narrow, narrow, jax.ShapeDtypeStruct((heads, DK), f32), jax.ShapeDtypeStruct((DK, width), bf16),
        ],
        scratch_shapes=[pltpu.VMEM((DK, width), f32)],
        compiler_params=pltpu.CompilerParams(
            dimension_semantics=("arbitrary",), vmem_limit_bytes=VMEM_LIMIT
        ),
        cost_estimate=cost(length * width * 128 * 10, length * width * 24),
        name="back_span",
    )(cols, rows, grad, out, gate_lin, head_gain, q, k, score, w)


def back_kernel(
    heads, chips, place_ref, all_ref, grads_ref, cols_ref, rows_ref, mixed_ref, q_ref, k_ref, v_ref,
    out_grad_ref, inv_ref, score_ref, w_ref, delta_ref, start_ref,
    mixed_grad_ref, col_grad_ref, row_grad_ref, state_ref,
):
    step = pl.program_id(0)
    row, col = places()
    width = heads * DK

    @pl.when(step == 0)
    def _():
        state_ref[...] = jnp.zeros_like(state_ref)

        def join(turn, carry):
            slot = place_ref[RING_AT + 3 * chips - 1 - turn]
            for h in range(heads):
                move = all_ref[slot, :, (2 * h + 1) * DK : 2 * (h + 1) * DK]
                state = state_ref[:, lanes(h)].astype(bf16)
                state_ref[:, lanes(h)] = tm(move, state) + grads_ref[slot, :, lanes(h)].astype(f32)
            return carry

        lax.fori_loop(0, chips - 1 - place_ref[CHIP_AT], join, 0)

    cols, rows = cols_ref[...], rows_ref[...]
    mixed = mixed_ref[...]
    at_or_after = row >= col
    by_col, by_row = running_sums(cols, rows[:8], at_or_after)
    same = cols[:, DOC_AT : DOC_AT + 1] == rows[8:9, :]
    inclusive = same & at_or_after
    strict = row > col
    lane = lax.broadcasted_iota(jnp.int32, (CHUNK, LANES), 1)
    last = lax.broadcasted_iota(jnp.int32, (CHUNK, 1), 0) == CHUNK - 1
    sub = lax.broadcasted_iota(jnp.int32, (8, CHUNK), 0)
    gate_cols = jnp.zeros((CHUNK, LANES), f32)
    beta_cols = jnp.zeros((CHUNK, LANES), f32)
    gate_rows = jnp.zeros((8, CHUNK), f32)
    rowsum = lambda a: jnp.sum(a, axis=-1, keepdims=True)
    for h in range(heads):
        q, k, v = q_ref[:, lanes(h)], k_ref[:, lanes(h)], v_ref[:, lanes(h)]
        q32, k32, v32 = q.astype(f32), k.astype(f32), v.astype(f32)
        out_grad, inv, score = out_grad_ref[:, lanes(h)], inv_ref[:, lanes(h)], score_ref[:, lanes(h)]
        w, delta, start = w_ref[:, lanes(h)], delta_ref[:, lanes(h)], start_ref[:, lanes(h)]
        beta = cols[:, BETA_AT + h : BETA_AT + h + 1]
        entry, tail = entry_and_tail(by_col, cols, h)
        gamma = ratios(by_col, by_row, h, inclusive)
        lower = jnp.where(strict, gamma * mt(k, k), 0.0)
        state = state_ref[:, lanes(h)]
        state16 = state.astype(bf16)
        key_tail = (k32 * tail).astype(bf16)
        query_entry = (q32 * entry).astype(bf16)
        delta_grad = (tm(score, out_grad) + mm(key_tail, state16)).astype(bf16)
        target_grad = tm(inv, delta_grad)
        target_grad16 = target_grad.astype(bf16)
        score_grad = mt(out_grad, delta)
        lower_grad = -mt(target_grad16, delta)
        out_state = mt(out_grad, start)
        target_state = mt(target_grad16, start)
        tail_grad = mt(delta, state16)
        score_part = (score_grad * gamma).astype(bf16)
        scaled = jnp.where(strict, lower_grad * gamma * beta, 0.0).astype(bf16)
        q_grad = entry * out_state + mm(score_part, k)
        k_grad = (
            tm(score_part, q) + tail * tail_grad - (beta * entry) * target_state
            + mm(scaled, k) + tm(scaled, k)
        )
        v_grad = beta * target_grad
        state_ref[:, lanes(h)] = (
            entry[CHUNK - 1 :, :] * state + tm(query_entry, out_grad) - tm(w, delta_grad)
        )
        lower_part = lower_grad * lower
        through = score_grad * score.astype(f32) + beta * lower_part
        entry_part = rowsum(target_state * k32) * entry
        tail_part = rowsum(tail_grad * k32) * tail
        carried = jnp.sum(rowsum(start.astype(f32) * state), axis=0, keepdims=True)
        at_end = jnp.sum(tail_part, axis=0, keepdims=True) + entry[CHUNK - 1 :, :] * carried
        gate_col = rowsum(through) + entry * rowsum(out_state * q32) - beta * entry_part - tail_part
        gate_col = gate_col + jnp.where(last, at_end, 0.0)
        beta_col = rowsum(target_grad * v32) - entry_part + rowsum(lower_part)
        gate_cols = jnp.where(lane == h, gate_col, gate_cols)
        beta_cols = jnp.where(lane == BETA_AT + h, beta_col, beta_cols)
        gate_rows = jnp.where(sub == h, jnp.sum(through, axis=0, keepdims=True), gate_rows)
        raw, gates, active, scales = activate(mixed, width, h)
        grads = []
        for part, grad in enumerate((q_grad, k_grad)):
            unit = active[part] * scales[part]
            grads.append(scales[part] * (grad - unit * rowsum(grad * unit)))
        grads.append(v_grad)
        for part in range(3):
            slope = gates[part] * (1.0 + raw[part] * (1.0 - gates[part]))
            at = part * width + h * DK
            mixed_grad_ref[:, at : at + DK] = grads[part] * slope
    exact = lax.Precision.HIGHEST
    tril = at_or_after.astype(f32)
    summed = lax.dot_general(
        tril, gate_cols, (((0,), (0,)), ((), ())), precision=exact, preferred_element_type=f32
    )
    col_grad_ref[...] = summed + beta_cols
    row_grad_ref[...] = jnp.dot(gate_rows, tril, precision=exact, preferred_element_type=f32)


def run_back(place, gathered, grads, cols, rows, mixed, q, k, v, out_grad, inv, score, w, delta, start):
    length, width = q.shape
    heads = width // DK
    count = length // CHUNK
    spec = lambda w: pl.BlockSpec((CHUNK, w), lambda i, p: (count - 1 - i, 0))
    whole = lambda shape: pl.BlockSpec(shape, lambda i, p: (0, 0, 0))
    return pl.pallas_call(
        partial(back_kernel, heads, gathered.shape[0]),
        grid_spec=pltpu.PrefetchScalarGridSpec(
            num_scalar_prefetch=1,
            grid=(count,),
            in_specs=[
                whole(gathered.shape), whole(grads.shape), spec(LANES),
                pl.BlockSpec((16, CHUNK), lambda i, p: (0, count - 1 - i)),
                spec(3 * width),
            ] + [spec(width)] * 9,
            out_specs=[
                spec(3 * width), spec(LANES), pl.BlockSpec((8, CHUNK), lambda i, p: (0, count - 1 - i)),
            ],
            scratch_shapes=[pltpu.VMEM((DK, width), f32)],
        ),
        out_shape=[
            jax.ShapeDtypeStruct((length, 3 * width), f32),
            jax.ShapeDtypeStruct((length, LANES), f32),
            jax.ShapeDtypeStruct((8, length), f32),
        ],
        compiler_params=pltpu.CompilerParams(
            dimension_semantics=("arbitrary",), vmem_limit_bytes=VMEM_LIMIT
        ),
        cost_estimate=cost(length * width * 128 * 36, length * width * 40),
        name="span_backward",
    )(place, gathered, grads, cols, rows, mixed, q, k, v, out_grad, inv, score, w, delta, start)


def half_columns(weights, table):
    half = weights.shape[2] // 2
    if half % LANES == 0:
        return weights, CORE_AT, half
    return lax.dynamic_slice_in_dim(weights, table[CORE_AT] * half, half, 2), ZERO_AT, half


def into_columns_kernel(place_ref, x_ref, w_ref, out_ref):
    out_ref[...] = mm(x_ref[...], w_ref[...]).astype(out_ref.dtype)


def into_columns(x, weights, table, first, count, kind=f32):
    weights, at, half = half_columns(weights, table)
    length, depth = x.shape
    wide = count * half
    return pl.pallas_call(
        into_columns_kernel,
        grid_spec=pltpu.PrefetchScalarGridSpec(
            num_scalar_prefetch=1,
            grid=(count,),
            in_specs=[
                pl.BlockSpec(x.shape, lambda j, p: (0, 0)),
                pl.BlockSpec((None, depth, half), lambda j, p: (first + j, 0, p[at])),
            ],
            out_specs=pl.BlockSpec((length, half), lambda j, p: (0, j)),
        ),
        out_shape=jax.ShapeDtypeStruct((length, wide), kind),
        compiler_params=pltpu.CompilerParams(
            dimension_semantics=("arbitrary",), vmem_limit_bytes=VMEM_LIMIT
        ),
        cost_estimate=cost(2 * length * depth * wide, 2 * (length * depth + depth * wide) + 4 * length * wide),
        name="into_columns",
    )(table, x, weights)


def from_columns_kernel(steps, place_ref, g_ref, w_ref, out_ref, *total):
    term = mt(w_ref[...], g_ref[...])
    if steps == 1:
        out_ref[...] = term.T.astype(out_ref.dtype)
        return
    total_ref, step = total[0], pl.program_id(0)

    @pl.when(step == 0)
    def _():
        total_ref[...] = term

    @pl.when((step > 0) & (step < steps - 1))
    def _():
        total_ref[...] += term

    @pl.when(step == steps - 1)
    def _():
        out_ref[...] = (total_ref[...] + term).T.astype(out_ref.dtype)


def from_columns(g, weights, table, first, row_at, length, kind=f32):
    weights, at, half = half_columns(weights, table)
    wide = g.shape[1]
    depth = weights.shape[1]
    steps = wide // half
    if half % LANES:
        g = lax.dynamic_slice_in_dim(g, table[row_at] * length, length, 0)
        parts = [dot_t(g[:, m * half : (m + 1) * half], weights[first + m]) for m in range(steps)]
        return sum(parts).astype(kind)
    return pl.pallas_call(
        partial(from_columns_kernel, steps),
        grid_spec=pltpu.PrefetchScalarGridSpec(
            num_scalar_prefetch=1,
            grid=(steps,),
            in_specs=[
                pl.BlockSpec((length, half), lambda j, p: (p[row_at], j)),
                pl.BlockSpec((None, depth, half), lambda j, p: (first + j, 0, p[at])),
            ],
            out_specs=pl.BlockSpec((length, depth), lambda j, p: (0, 0)),
            scratch_shapes=[pltpu.VMEM((depth, length), f32)] if steps > 1 else [],
        ),
        out_shape=jax.ShapeDtypeStruct((length, depth), kind),
        compiler_params=pltpu.CompilerParams(
            dimension_semantics=("arbitrary",), vmem_limit_bytes=VMEM_LIMIT
        ),
        cost_estimate=cost(2 * length * depth * wide, 2 * (length * wide + depth * wide) + 4 * length * depth),
        name="from_columns",
    )(table, g, weights)


def feed_kernel(place_ref, x_ref, cot_ref, w_ref, hidden_ref, pair_ref, gate_ref, up_ref):
    step = pl.program_id(0)
    half = hidden_ref.shape[1]

    @pl.when(step == 0)
    def _():
        gate_ref[...] = mm(x_ref[...], w_ref[...])

    @pl.when(step == 1)
    def _():
        up = mm(x_ref[...], w_ref[...])
        gate = gate_ref[...]
        up_ref[...] = up
        hidden_ref[...] = (gate * sigmoid(gate) * up).astype(bf16)

    @pl.when(step == 2)
    def _():
        grad = mm(cot_ref[...], w_ref[...])
        gate, up = gate_ref[...], up_ref[...]
        sig = sigmoid(gate)
        pair_ref[:, :half] = (grad * up * (sig * (1.0 + gate * (1.0 - sig)))).astype(bf16)
        pair_ref[:, half:] = (grad * (gate * sig)).astype(bf16)


def run_feed(x, cot, weights, table):
    weights, at, half = half_columns(weights, table)
    length, depth = x.shape
    fixed = lambda a: pl.BlockSpec(a.shape, lambda j, p: (0, 0))
    whole = lambda wide: pl.BlockSpec((length, wide), lambda j, p: (0, 0))
    return pl.pallas_call(
        feed_kernel,
        grid_spec=pltpu.PrefetchScalarGridSpec(
            num_scalar_prefetch=1,
            grid=(3,),
            in_specs=[fixed(x), fixed(cot), pl.BlockSpec((None, depth, half), lambda j, p: (j, 0, p[at]))],
            out_specs=[whole(half), whole(2 * half)],
            scratch_shapes=[pltpu.VMEM((length, half), f32)] * 2,
        ),
        out_shape=[jax.ShapeDtypeStruct((length, half), bf16), jax.ShapeDtypeStruct((length, 2 * half), bf16)],
        compiler_params=pltpu.CompilerParams(
            dimension_semantics=("arbitrary",), vmem_limit_bytes=VMEM_LIMIT
        ),
        cost_estimate=cost(6 * length * depth * half, 6 * depth * half),
        name="feed",
    )(table, x, cot, weights)


def ring_step_kernel(arrived, place_ref, *refs):
    left = jnp.concatenate([refs[0][...], refs[1][...]], 1)
    term = tm(left, refs[2][...])
    rows = refs[0].shape[1]
    for way in range(2):
        part = term[way * rows : (way + 1) * rows]
        if arrived:
            part = part + refs[3 + way][...].astype(f32)
        out = refs[3 + 2 * arrived + way]
        out[...] = part.astype(out.dtype)


def ring_step(left, right, table, step, arrived, rows, kind):
    length, wide = right.shape
    if rows % LANES:
        sums = []
        for way in range(2):
            strip = lax.dynamic_slice_in_dim(left, table[RING_AT + 2 * step + way] * rows, rows, 1)
            term = lax.dot_general(strip, right, (((0,), (0,)), ((), ())), preferred_element_type=f32)
            sums.append((term + arrived[way].astype(f32) if arrived else term).astype(kind))
        return sums
    tile = max([t for t in range(LANES, 1409, LANES) if wide % t == 0] or [wide])
    strip = lambda way: pl.BlockSpec((length, rows), lambda j, p: (0, p[RING_AT + 2 * step + way]))
    tiled = lambda height: pl.BlockSpec((height, tile), lambda j, p: (0, j))
    return pl.pallas_call(
        partial(ring_step_kernel, 1 if arrived else 0),
        grid_spec=pltpu.PrefetchScalarGridSpec(
            num_scalar_prefetch=1,
            grid=(wide // tile,),
            in_specs=[strip(0), strip(1), tiled(length)] + [tiled(rows)] * len(arrived),
            out_specs=[tiled(rows)] * 2,
        ),
        out_shape=[jax.ShapeDtypeStruct((rows, wide), kind)] * 2,
        compiler_params=pltpu.CompilerParams(
            dimension_semantics=("arbitrary",), vmem_limit_bytes=VMEM_LIMIT
        ),
        cost_estimate=cost(4 * length * rows * wide, 2 * length * wide + 8 * rows * wide),
        name="ring_step",
    )(table, left, left, right, *arrived)


def norm_rows(value, gain):
    return value * lax.rsqrt(jnp.mean(value * value, axis=-1, keepdims=True) + epsilon) * gain


def doc_index(positions, starts):
    return jnp.sum((positions[..., None] >= starts).astype(jnp.int32), axis=-1) - 1


def swish_product(gate, up):
    return jax.nn.silu(gate) * up


def dot(a, b):
    return jnp.dot(a, b, preferred_element_type=f32)


def dot_t(a, b):
    return lax.dot_general(a, b, (((1,), (1,)), ((), ())), preferred_element_type=f32)


def ring_of(chips):
    rows = max(1, chips // 4)
    if rows < 2 or chips % rows:
        return list(range(chips))
    depth = chips // rows
    order = [z * rows for z in range(depth)]
    for z in range(depth - 1, -1, -1):
        line = [z * rows + y for y in range(1, rows)]
        order += line if (depth - 1 - z) % 2 == 0 else line[::-1]
    return order


def shards(
    tokens, cotangent, norm_gains, mix_weight, rate_weight, feed_weight, conv_weight,
    decay_log, decay_bias, head_gain, doc_starts,
):
    count, model = tokens.shape
    spans = lax.axis_size("seq")
    chips = spans // 2
    tensors = lax.axis_size("tensor")
    place = lax.axis_index("seq")
    core = lax.rem(place, 2)
    chip = lax.div(place, 2)
    first_core = core == 0
    rows = mix_weight.shape[0]
    heads_all = decay_log.shape[0]
    heads = heads_all // 2
    width = heads * DK
    hidden_width = feed_weight.shape[2] // 2
    length = 2 * count
    reach = conv_weight.shape[0]
    ring = ring_of(chips)
    ring_place = [ring.index(c) for c in range(chips)]
    my_ring = jnp.asarray(ring_place, jnp.int32)[chip]

    toward = jnp.arange(chips, dtype=jnp.int32)
    ring_table = jnp.asarray(ring, jnp.int32)
    owners = [
        2 * ring_table[lax.rem(my_ring - way * (1 + toward) + 2 * chips, chips)] + half
        for way, half in ((1, 0), (-1, 1))
    ]
    slots = lax.rem(my_ring - jnp.asarray(ring_place, jnp.int32) + chips, chips)
    table = jnp.concatenate(
        [jnp.stack([core, 1 - core, 0 * core, 0 * core + 1, chip]), jnp.stack(owners, 1).reshape(-1), slots]
    ).astype(jnp.int32)

    turn = []

    def in_turn(*arrays):
        if not turn:
            return list(arrays)
        return list(lax.optimization_barrier((*arrays, turn[-1]))[: len(arrays)])

    def done(array):
        turn.append(array)

    def core_swap(a):
        return lax.ppermute(a, "seq", [(i, i ^ 1) for i in range(spans)])

    def ring_shift(a, by):
        pairs = [
            (2 * ring[i] + k, 2 * ring[(i + by) % chips] + k) for i in range(chips) for k in range(2)
        ]
        return lax.ppermute(a, "seq", pairs)

    def chip_swap(a, distance):
        return lax.ppermute(a, "seq", [(i, i ^ (2 * distance)) for i in range(spans)])

    def chips_sum(a):
        distance = 1
        while distance < chips:
            a = a + chip_swap(a, distance)
            distance *= 2
        return a

    def tensor_sum(a):
        a = a.astype(bf16)
        if tensors == 2:
            return a.astype(f32) + lax.ppermute(a, "tensor", [(0, 1), (1, 0)]).astype(f32)
        return lax.psum(a, "tensor").astype(f32)

    def ring_gather(a):
        held = [a] + [None] * (chips - 1)
        up = down = a
        for hop in range(1, chips // 2 + 1):
            up = ring_shift(up, 1)
            held[hop] = up
            if hop < chips - hop:
                down = ring_shift(down, -1)
                held[chips - hop] = down
        return jnp.stack(held)

    def mine_first(a):
        return jnp.where(first_core, a, jnp.concatenate([a[count:], a[:count]], 0))

    def in_order(own, other):
        return jnp.where(
            first_core, jnp.concatenate([own, other], 0), jnp.concatenate([other, own], 0)
        )

    mix_all = lax.all_gather(mix_weight.swapaxes(0, 1), "seq", axis=1, tiled=True)
    feed_all = lax.all_gather(feed_weight.swapaxes(0, 1), "seq", axis=1, tiled=True)

    rate_part = lambda at: lax.dynamic_slice_in_dim(rate_weight, at * heads, heads, 2).reshape(rows, 2 * heads).T
    rate_own, rate_other = rate_part(core), core_swap(rate_part(1 - core))
    rate_rows = jnp.where(
        first_core, jnp.concatenate([rate_own, rate_other], 1), jnp.concatenate([rate_other, rate_own], 1)
    )
    distance = 1
    while distance < chips:
        arrived = chip_swap(rate_rows, distance)
        rate_rows = jnp.where(
            (chip & distance) == 0,
            jnp.concatenate([rate_rows, arrived], 1),
            jnp.concatenate([arrived, rate_rows], 1),
        )
        distance *= 2

    seq_count = doc_starts.shape[0]
    seq_len = count * spans // seq_count
    starts = (doc_starts + jnp.arange(seq_count, dtype=jnp.int32)[:, None] * seq_len).reshape(-1)
    positions = chip * length + jnp.arange(length, dtype=jnp.int32)
    documents = doc_index(positions, starts)
    lagged = doc_index(positions[:, None] - jnp.arange(reach, dtype=jnp.int32)[None, :], starts)
    link = (lagged == documents[:, None]).astype(f32)
    by_chunk = documents.reshape(-1, CHUNK)
    before = doc_index(positions[::CHUNK] - 1, starts)
    carry = (by_chunk == before[:, None]).astype(f32).reshape(length)
    tail = (by_chunk == by_chunk[:, -1:]).astype(f32).reshape(length)

    other_tokens = core_swap(tokens)
    cot_other = core_swap(cotangent)
    edge = tokens[count - HALO :]
    halo = lax.ppermute(edge, "seq", [(2 * c + 1, 2 * c + 2) for c in range(chips - 1)])
    halo = halo + lax.ppermute(edge, "seq", [(2 * c + 1, 2 * c + 3) for c in range(chips - 1)])
    chip_tokens = jnp.concatenate([halo, in_order(tokens, other_tokens)], 0).astype(f32)
    normed_halo = norm_rows(chip_tokens, norm_gains[0]).astype(bf16)
    normed = normed_halo[HALO:]
    inputs = tokens.astype(f32)
    cot = jnp.concatenate([cotangent, cot_other], 0)
    _, norm_first_back = jax.vjp(norm_rows, inputs, norm_gains[0])

    padded = into_columns(normed_halo, mix_all, table, 0, 3, bf16).astype(f32)
    rates = dot_t(normed, rate_rows)
    gate_lin = into_columns(normed, mix_all, table, 3, 1)
    own_taps = lax.dynamic_slice_in_dim(
        conv_weight.reshape(reach, 3, 2, width), core, 1, 2
    ).reshape(reach, 3 * width)
    own = lambda a: lax.dynamic_slice_in_dim(a, core * heads, heads, 0)
    log_scale, bias, gain = own(decay_log), own(decay_bias), own(head_gain)

    def convolve(padded, taps):
        mixed = taps[0] * padded[HALO:] * link[:, 0:1]
        for tap in range(1, reach):
            mixed = mixed + taps[tap] * padded[HALO - tap : HALO - tap + length] * link[:, tap : tap + 1]
        return mixed

    def gates(rates, log_scale, bias):
        log_gate = -jnp.exp(log_scale) * jax.nn.softplus(rates[:, :heads] + bias)
        return log_gate, jax.nn.sigmoid(rates[:, heads:])

    mixed, convolve_back = jax.vjp(convolve, padded, own_taps)
    (log_gate, beta), gates_back = jax.vjp(gates, rates, log_scale, bias)
    doc_parts = jnp.stack([documents.astype(f32), carry, tail], 1)
    cols = jnp.concatenate(
        [
            jnp.pad(log_gate, ((0, 0), (0, BETA_AT - heads))),
            jnp.pad(beta, ((0, 0), (0, DOC_AT - BETA_AT - heads))),
            jnp.pad(doc_parts, ((0, 0), (0, LANES - DOC_AT - 3))),
        ],
        1,
    )
    by_rows = jnp.concatenate(
        [jnp.pad(log_gate.T, ((0, 8 - heads), (0, 0))), jnp.broadcast_to(documents.astype(f32), (8, length))],
        0,
    )
    q, k, v, out0, reached, inverse, score, w, delta2, start2, final = run_span(cols, by_rows, mixed, heads)
    gathered = ring_gather(final)
    gated, mixer_out, delta, start = run_enter(
        table, gathered, out0, reached, delta2, start2, gate_lin, gain
    )
    arrived = core_swap(from_columns(gated, mix_all, table, 4, OTHER_AT, count, bf16))
    middle = inputs + tensor_sum(from_columns(gated, mix_all, table, 4, CORE_AT, count) + arrived.astype(f32))
    normed2_own32, norm_second_back = jax.vjp(norm_rows, middle, norm_gains[1])
    normed2_own = normed2_own32.astype(bf16)

    normed2 = jnp.concatenate([normed2_own, core_swap(normed2_own)], 0)
    hidden, pair_grad = run_feed(normed2, cot, feed_all, table)

    def advance(stream):
        left, right, arrived, step = stream
        if step == chips:
            return
        if arrived:
            arrived = in_turn(*arrived)
        else:
            (right,) = in_turn(right)
        last = step == chips - 1
        sums = ring_step(left, right, table, step, arrived, rows, f32 if last else bf16)
        done(sums[0])
        arrived = sums if last else [ring_shift(sums[0], 1), ring_shift(sums[1], -1)]
        stream[2:] = [arrived, step + 1]

    def finish(stream):
        up, down = stream[2]
        keep = jnp.where(first_core, up, down)
        return keep, core_swap(jnp.where(first_core, down, up).astype(bf16)).astype(f32)

    down_stream, pair_stream = [cot, hidden, [], 0], [normed2, pair_grad, [], 0]

    def halves_sum(a, first):
        (a,) = in_turn(a)
        theirs = from_columns(a, feed_all, table, first, ONE_AT, count, bf16)
        done(theirs)
        arrived = core_swap(theirs)
        (a,) = in_turn(a)
        own = from_columns(a, feed_all, table, first, ZERO_AT, count)
        done(own)
        return tensor_sum(own + arrived.astype(f32))

    def feed_ring():
        advance(down_stream)
        advance(pair_stream)

    feed_ring()
    second_grad = halves_sum(pair_grad, 0)
    feed_ring()
    branch = halves_sum(hidden, 2)
    block_out = (middle + branch).astype(bf16)
    feed_ring()

    (second_grad,) = in_turn(second_grad)
    middle_norm_grad, gain_second_grad = norm_second_back(second_grad)
    middle_grad = cot[:count].astype(f32) + middle_norm_grad
    attended_grad_own = middle_grad.astype(bf16)
    attended_grad = in_order(attended_grad_own, core_swap(attended_grad_own))
    gated_grad = into_columns(attended_grad, mix_all, table, 4, 1)
    out_grad, gate_lin_grad, head_gain_grad, local_grad = run_back_span(
        cols, by_rows, gated_grad, mixer_out, gate_lin, gain, q, k, score, w
    )
    done(local_grad)
    feed_ring()
    state_grads = ring_gather(local_grad)
    feed_ring()
    (state_grads,) = in_turn(state_grads)
    mixed_grad, col_grads, row_grads = run_back(
        table, gathered, state_grads, cols, by_rows, mixed, q, k, v, out_grad, inverse, score, w, delta, start
    )
    done(col_grads)
    feed_ring()
    mixed_grad, col_grads = in_turn(mixed_grad, col_grads)
    log_gate_grad = col_grads[:, :heads] - row_grads[:heads].T
    beta_grad = col_grads[:, BETA_AT : BETA_AT + heads]
    rates_grad, log_scale_grad, bias_grad = gates_back((log_gate_grad, beta_grad))
    padded_grad, taps_grad = convolve_back(mixed_grad)
    returned = lax.ppermute(
        padded_grad[:HALO],
        "seq",
        [(2 * c + k, 2 * c - 2 + k) for c in range(1, chips) for k in range(2)],
    )
    pre_grad = padded_grad[HALO:].at[length - HALO :].add(returned)
    projected_grad = jnp.concatenate([pre_grad.astype(bf16), gate_lin_grad], 1)
    own_rates = lax.dynamic_slice_in_dim(rates_grad, core * count, count, 0).astype(bf16)
    other_rates = lax.dynamic_slice_in_dim(rates_grad, (1 - core) * count, count, 0).astype(bf16)


    out_stream, mix_stream = [attended_grad, gated, [], 0], [normed, projected_grad, [], 0]

    def mix_ring():
        advance(mix_stream)
        advance(out_stream)

    mix_ring()
    feed_ring()

    def first_part(row_at, rates):
        (grad,) = in_turn(projected_grad)
        part = from_columns(grad, mix_all, table, 0, row_at, count)
        done(part)
        return part + dot(rates, rate_rows)

    arrived = core_swap(first_part(OTHER_AT, other_rates).astype(bf16))
    first_grad = tensor_sum(first_part(CORE_AT, own_rates) + arrived.astype(f32))
    mix_ring()
    feed_ring()
    for _ in range(chips):
        feed_ring()
    down_sum, pair_sums = finish(down_stream), finish(pair_stream)
    for _ in range(chips):
        mix_ring()
    mix_sum, out_sum = finish(mix_stream), finish(out_stream)
    token_norm_grad, gain_first_grad = norm_first_back(first_grad)
    token_gradient = middle_grad + token_norm_grad
    rate_sum = lax.dot_general(
        rates_grad, normed.astype(f32), (((0,), (0,)), ((), ())), precision=lax.Precision.HIGHEST
    )

    def both_halves(own, other):
        return jnp.where(first_core, jnp.concatenate([own, other], 2), jnp.concatenate([other, own], 2))

    shape = lambda a, parts: a.reshape(rows, parts, -1)
    mix_gradient = both_halves(
        *[
            jnp.concatenate([shape(a, 4), shape(b, 1)], 1) for a, b in zip(mix_sum, out_sum)
        ]
    )
    feed_gradient = both_halves(
        *[jnp.concatenate([shape(a, 2), shape(b, 1)], 1) for a, b in zip(pair_sums, down_sum)]
    )

    gains_grad = jnp.stack([gain_first_grad, gain_second_grad])
    small = [taps_grad.reshape(reach, 3, width), log_scale_grad, bias_grad, head_gain_grad]
    small += [rate_sum.reshape(2, heads, model), gains_grad]
    flat = jnp.concatenate([a.reshape(-1) for a in small])
    flat = chips_sum(jnp.pad(flat, (0, -flat.size % 1024)).reshape(-1, LANES))
    flat_other = core_swap(flat)
    first, second = jnp.where(first_core, flat, flat_other), jnp.where(first_core, flat_other, flat)
    first, second = first.reshape(-1), second.reshape(-1)
    summed, at = [], 0
    for a, axis in zip(small, (2, 0, 0, 0, 1, None)):
        sides = [side[at : at + a.size].reshape(a.shape) for side in (first, second)]
        summed.append(sides[0] + sides[1] if axis is None else jnp.concatenate(sides, axis))
        at += a.size
    rate_gradient = lax.dynamic_slice_in_dim(summed[4], place * rows, rows, 2).transpose(2, 0, 1)
    return (
        block_out, token_gradient, summed[5], mix_gradient, rate_gradient, feed_gradient,
        summed[0], summed[1], summed[2], summed[3],
    )


def solution(mesh):
    return jax.shard_map(
        shards,
        mesh=mesh,
        in_specs=(
            P("seq", None),
            P("seq", None),
            P(),
            P("seq", None, "tensor"),
            P("seq", None, "tensor"),
            P("seq", None, "tensor"),
            P(None, None, "tensor"),
            P("tensor"),
            P("tensor"),
            P("tensor", None),
            P(),
        ),
        out_specs=(
            P("seq", None),
            P("seq", None),
            P(),
            P("seq", None, "tensor"),
            P("seq", None, "tensor"),
            P("seq", None, "tensor"),
            P(None, None, "tensor"),
            P("tensor"),
            P("tensor"),
            P("tensor", None),
        ),
        check_vma=False,
    )
```
